32 devices in a mesh: gx: 4 (over y, core), gy: 8 (over z, x).
Axes of the slice: x: 2, y: 2, z: 4, core: 2. Of those that a mesh axis runs over, the one named last changes fastest.
Arguments:
- positions: float32 [3, 1024, 4096], P(None, 'gx', 'gy'), may hold values from -6 to 6
- velocity: float32 [3, 1024, 4096], P(None, 'gx', 'gy'), may hold values from -3 to 3
- stiffness: float32 [1024, 4096], P('gx', 'gy'), may hold values from 0.5 to 4
- send_tiles: int32 [4, 8, 128], P('gx', 'gy'), may hold values from -1 to 1023, as said below
- pair_tiles: int32 [4, 8, 2, 256], P('gx', 'gy'), may hold values from -1 to 127, as said below
Outputs:
- new_positions: float32 [3, 1024, 4096], P(None, 'gx', 'gy')
- new_velocity: float32 [3, 1024, 4096], P(None, 'gx', 'gy')
The draws below stay inside these ranges and needn't reach their ends.
Inputs may be any that keep to these rules, and one draw needn't show every extreme that they name: `send_tiles`: entry o * 4 + k of a device names the patch tile in slot k towards owner o, -1 marking an empty slot; the filled slots towards an owner come first, and some owner receives all 4 slots filled from every device. `pair_tiles`: at each owner, column m is a face-pair tile: its two rows name two different filled received slots, slot s * 4 + k being slot k sent to this owner by owner s. Unused columns hold -1 in both rows and follow the used ones; some owner uses all 256 columns.
All inputs are finite; a program needn't handle non-finite values.
Results may differ from the reference program's by a relative error of at most 0.0003.
Values sent between devices are 32-bit elements; how exact they have to be, the bound alone decides.
A program may use at most 64 MiB of HBM per device.

```python
import math
import jax
import jax.numpy as jnp
from jax import lax

PR = 256
PC = 512
TILE = 128
SLOTS = 4
PMAX = 256
STEPS = 2
TILES = 1024
NR = 1024
NC = 4096
N_GX = 4
N_GY = 8


def contact_plan(key):
    folded = jax.random.fold_in(key, 7)
    key_counts, key_full = jax.random.split(folded, 2)
    owners = N_GX * N_GY
    counts = jax.random.randint(key_counts, (owners, owners), 0, SLOTS + 1)
    full_owner = jax.random.randint(key_full, (), 0, owners)
    source = jnp.arange(owners)[:, None]
    target = jnp.arange(owners)[None, :]
    counts = jnp.where(target == full_owner, SLOTS, counts)
    counts = jnp.where(source == target, SLOTS, counts)
    counts = jnp.where(source == (target + 1) % owners, jnp.maximum(counts, 1), counts)
    empty_target = (full_owner + 1) % owners
    empty_source = (empty_target + 2) % owners
    counts = jnp.where((source == empty_source) & (target == empty_target), 0, counts)
    return (counts, full_owner)


def draw_send_tiles(key, part):
    counts, full_owner = contact_plan(key)
    owners = N_GX * N_GY
    chosen = jax.random.randint(jax.random.fold_in(key, 11), (owners, owners, SLOTS), 0, TILES)
    chosen = chosen.at[0, full_owner, 0].set(TILES - 1)
    filled = jnp.arange(SLOTS)[None, None, :] < counts[:, :, None]
    return jnp.where(filled, chosen, -1).reshape(N_GX, N_GY, owners * SLOTS).astype(jnp.int32)


def draw_pair_tiles(key, part):
    counts, full_owner = contact_plan(key)
    owners = N_GX * N_GY
    subkeys = jax.random.split(jax.random.fold_in(key, 13), 3)
    arrived = counts.T
    cumulative = jnp.cumsum(arrived, axis=1)
    totals = cumulative[:, -1]
    first_pick = jax.random.randint(subkeys[0], (owners, PMAX), 0, totals[:, None])
    other_pick = jax.random.randint(subkeys[1], (owners, PMAX), 0, totals[:, None] - 1)
    second_pick = (first_pick + 1 + other_pick) % totals[:, None]

    def slot_of(picks):
        sender = jnp.sum((cumulative[:, None, :] <= picks[:, :, None]).astype(jnp.int32), axis=2)
        before = jnp.take_along_axis(cumulative - arrived, sender, axis=1)
        return sender * SLOTS + picks - before
    first_slot = slot_of(first_pick)
    second_slot = slot_of(second_pick)
    shifts = jax.random.randint(subkeys[2], (owners,), 0, 4)
    in_use = PMAX // 2 ** shifts
    in_use = in_use.at[(full_owner + 1) % owners].set(PMAX // 8)
    in_use = in_use.at[full_owner].set(PMAX)
    active = jnp.arange(PMAX)[None, :] < in_use[:, None]
    first_slot = jnp.where(active, first_slot, -1).at[full_owner, 0].set(owners * SLOTS - 1)
    second_slot = jnp.where(active, second_slot, -1).at[full_owner, 0].set(0)
    paired = jnp.stack([first_slot, second_slot], axis=1)
    return paired.reshape(N_GX, N_GY, 2, PMAX).astype(jnp.int32)


def levels(rng, extent, pieces, least, top_value):
    def one(position, blocks):
        steps = jax.random.uniform(jax.random.fold_in(jax.random.fold_in(rng, 6), position), (blocks,), jnp.float32, least / len(pieces), top_value / len(pieces))
        return jnp.repeat(jnp.exp(steps), extent[position] // blocks).reshape((-1,) + (1,) * (len(extent) - position - 1))

    gain = one(*pieces[0])
    for cut in pieces[1:]:
        gain = gain * one(*cut)
    return gain


def noise(key, shape, spread, bound, cuts=(), kind=jnp.bfloat16):
    drawn = spread * jax.random.normal(key, shape, jnp.float32)
    if cuts:
        drawn = drawn * levels(key, shape, cuts, -0.22, 0.18)
    return jnp.clip(drawn, -bound, bound).astype(kind)


def setup_inputs(seed: int = 0) -> dict:
    arg_keys = jax.random.split(jax.random.key(seed), 6)
    return {
        "positions": noise(arg_keys[0], (3, NR, NC), 1.0, 6.0, ((1, 4), (2, 8)), jnp.float32),
        "velocity": noise(arg_keys[1], (3, NR, NC), 0.5, 3.0, ((1, 4), (2, 8)), jnp.float32),
        "stiffness": jnp.clip(jnp.exp(math.log(4.0) - 2.0794415 * jax.random.uniform(arg_keys[2], (NR, NC), jnp.float32) ** levels(arg_keys[2], (NR, NC), ((0, 4), (1, 8)), -0.2, 0.2)), 0.5, 4.0),
        "send_tiles": draw_send_tiles(jax.random.fold_in(arg_keys[5], 71), 0),
        "pair_tiles": draw_pair_tiles(jax.random.fold_in(arg_keys[5], 71), 0),
    }


time_step = 0.1
damping = 0.2
hardening = 0.1
bend_gain = 0.02
contact_gain = 0.25
inverse_width = 0.5
block_rows = 32


def neighbours(padded):
    return (padded[:, 2:, 1:-1], padded[:, :-2, 1:-1], padded[:, 1:-1, 2:], padded[:, 1:-1, :-2])


def membrane(padded):
    center = padded[:, 1:-1, 1:-1]
    result = jnp.zeros(center.shape, jnp.float32)
    for beside in neighbours(padded):
        offset = beside - center
        result = result + offset * (1.0 + hardening * jnp.sum(offset * offset, axis=0, keepdims=True))
    return result


def laplace(padded):
    beside_all = neighbours(padded)
    return ((beside_all[0] + beside_all[1]) + (beside_all[2] + beside_all[3])) - 4.0 * padded[:, 1:-1, 1:-1]


def pad_grid(field):
    return jnp.pad(field, ((0, 0), (1, 1), (1, 1)))


def pair_block(near, far, active):
    offset = near[:, :, :, None] - far[:, :, None, :]
    weight = contact_gain * jnp.exp(-inverse_width * jnp.sum(offset * offset, axis=0)) * active[:, None, None]
    push = weight[None] * offset
    return jnp.sum(push, axis=3), -jnp.sum(push, axis=2)


def pair_forces(received, paired):
    first = paired[0]
    second = paired[1]
    active = (first >= 0).astype(jnp.float32)
    first_row = jnp.maximum(first, 0)
    second_row = jnp.maximum(second, 0)
    near = jnp.take(received, first_row, axis=1)
    far = jnp.take(received, second_row, axis=1)
    number = paired.shape[1]
    groups = number // block_rows

    def split_blocks(values):
        return jnp.moveaxis(values.reshape(3, groups, block_rows, values.shape[2]), 1, 0)

    def run_block(items):
        return pair_block(items[0], items[1], items[2])

    near_out, far_out = lax.map(run_block, (split_blocks(near), split_blocks(far), active.reshape(groups, block_rows)))
    near_force = jnp.moveaxis(near_out, 0, 1).reshape(3, number, received.shape[2])
    far_force = jnp.moveaxis(far_out, 0, 1).reshape(3, number, received.shape[2])
    return near_force, far_force, first_row, second_row, active


def owner_forces(received, paired):
    near_force, far_force, first_row, second_row, active = pair_forces(received, paired)
    result = jnp.zeros(received.shape, jnp.float32)
    result = result.at[:, first_row].add(near_force)
    return result.at[:, second_row].add(far_force)


def contact_force(positions, send_tiles, pair_tiles):
    owners = N_GX * N_GY
    per_device = positions.reshape(3, N_GX, PR, N_GY, PC).transpose(1, 3, 0, 2, 4).reshape(owners, 3, TILES, TILE)
    routes = send_tiles.reshape(owners, owners * SLOTS)

    def pick(patch, route):
        filled = (route >= 0).astype(jnp.float32)
        return jnp.take(patch, jnp.maximum(route, 0), axis=1) * filled[None, :, None]

    def swap_roles(blocks):
        return blocks.reshape(owners, 3, owners, SLOTS, TILE).transpose(2, 1, 0, 3, 4).reshape(owners, 3, owners * SLOTS, TILE)

    received = swap_roles(jax.vmap(pick)(per_device, routes))

    def at_owner(items):
        return owner_forces(items[0], items[1])

    slot_force = lax.map(at_owner, (received, pair_tiles.reshape(owners, 2, PMAX)))
    returned = swap_roles(slot_force)

    def deposit(route, values):
        filled = (route >= 0).astype(jnp.float32)
        return jnp.zeros((3, TILES, TILE), jnp.float32).at[:, jnp.maximum(route, 0)].add(values * filled[None, :, None])

    tiles = jax.vmap(deposit)(routes, returned)
    return tiles.reshape(N_GX, N_GY, 3, PR, PC).transpose(2, 0, 3, 1, 4).reshape(3, N_GX * PR, N_GY * PC)


def reference(positions, velocity, stiffness, send_tiles, pair_tiles):
    for repeat in range(STEPS):
        padded = pad_grid(positions)
        bend = laplace(pad_grid(laplace(padded)))
        force = stiffness[None] * membrane(padded) - bend_gain * bend + contact_force(positions, send_tiles, pair_tiles)
        velocity = velocity + time_step * (force - damping * velocity)
        positions = positions + time_step * velocity
    return positions, velocity
```

```python
import functools
import math

import jax
import jax.numpy as jnp
from jax import lax
from jax.experimental import pallas as pl
from jax.experimental.pallas import tpu as pltpu
from jax.sharding import PartitionSpec as P

TILE = 128
STEPS = 2
MESH = pl.DeviceIdType.MESH

time_step = 0.1
damping = 0.2
hardening = 0.1
bend_gain = 0.02
SCALE = math.sqrt(0.5 * math.log2(math.e))
CHUNK = 32
UNROLL = 4
bf16 = jnp.bfloat16
f32 = jnp.float32


def split3(x):
    hi = x.astype(bf16)
    rest = x - hi.astype(f32)
    mid = rest.astype(bf16)
    lo = (rest - mid.astype(f32)).astype(bf16)
    return hi, mid, lo


def kernel(ngx, ngy, slots, pos_ref, vel_ref, stiff_ref, route_s, route_v, pair_s, pair_v,
           pos_out, vel_out, xpad, blocks, force, sendbuf, recv, backsend, back, rec8, aug, pairsum,
           colsend, colrecv, rowrecv, cornrecv,
           tile_send, tile_recv, back_send, back_recv, halo_send, halo_recv):
    n = ngx * ngy
    rows, cols = pos_ref.shape[1], pos_ref.shape[2]
    wide = cols + TILE
    number = pair_s.shape[1]
    total = n * slots
    gi = lax.axis_index("gx")
    gj = lax.axis_index("gy")
    me = gi * ngy + gj

    def place(o):
        return (o // ngy, lax.rem(o, ngy))

    barrier = pltpu.get_barrier_semaphore()

    def greet(d, carry):
        pl.semaphore_signal(barrier, inc=1, device_id=place(lax.rem(me + d, n)), device_id_type=MESH)
        return carry

    lax.fori_loop(1, n, greet, 0)

    for c in range(3):
        xpad[c, 8:8 + rows, 0:cols] = pos_ref[c]
        for t in range(cols // TILE):
            blocks[t, c] = pos_ref[c, :, t * TILE:(t + 1) * TILE]
    vel_out[...] = vel_ref[...]
    rec8[...] = jnp.zeros_like(rec8)
    rec8[:, 3, :] = jnp.ones((total, TILE), f32)

    pl.semaphore_wait(barrier, n - 1)

    up = lax.rem(gi + ngx - 1, ngx)
    down = lax.rem(gi + 1, ngx)
    left = lax.rem(gj + ngy - 1, ngy)
    right = lax.rem(gj + 1, ngy)
    has_up = (gi > 0).astype(f32)
    has_down = (gi < ngx - 1).astype(f32)
    has_left = (gj > 0).astype(f32)
    has_right = (gj < ngy - 1).astype(f32)

    def tile_copy(step, o, source):
        return pltpu.make_async_remote_copy(
            src_ref=sendbuf.at[step, o], dst_ref=recv.at[step, source],
            send_sem=tile_send.at[step, o], recv_sem=tile_recv.at[step, source],
            device_id=place(o), device_id_type=MESH)

    def back_copy(step, o, source):
        return pltpu.make_async_remote_copy(
            src_ref=backsend.at[step, o], dst_ref=back.at[step, source],
            send_sem=back_send.at[step, o], recv_sem=back_recv.at[step, source],
            device_id=place(o), device_id_type=MESH)

    def run_step(step, carry):
        def fetch(o, put):
            for k in range(slots):
                at = k * n + o
                row = route_s[0, at]
                col = route_s[1, at]
                filled = (row >= 0).astype(f32)
                row = jnp.maximum(row, 0)
                col = jnp.maximum(col, 0)
                for c in range(3):
                    put(k * 3 + c, blocks[col, c, pl.ds(row, 1), :] * filled)

        def send_tiles(d, carry):
            o = lax.rem(me + d, n)

            def put(j, value):
                sendbuf[step, o, pl.ds(j, 1), :] = value

            fetch(o, put)
            tile_copy(step, o, me).start()
            return carry

        lax.fori_loop(1, n, send_tiles, 0)

        def put_own(j, value):
            recv[step, me, pl.ds(j, 1), :] = value

        fetch(me, put_own)

        lane = lax.broadcasted_iota(jnp.int32, (rows, TILE), 1)
        packed = jnp.zeros((rows, TILE), f32)
        for c in range(3):
            first = pltpu.roll(xpad[c, 8:8 + rows, 0:TILE], 2 * c, 1) if c else xpad[c, 8:8 + rows, 0:TILE]
            last = pltpu.roll(xpad[c, 8:8 + rows, cols - TILE:cols], 10 + 2 * c, 1)
            packed = jnp.where((lane == 2 * c) | (lane == 2 * c + 1), first, packed)
            packed = jnp.where((lane == 8 + 2 * c) | (lane == 9 + 2 * c), last, packed)
        turned = jnp.transpose(packed)
        colsend[step, 0] = turned[0:8]
        colsend[step, 1] = turned[8:16]

        top = pl.ds(8, 8)
        bottom = pl.ds(rows, 8)
        head = pl.ds(0, TILE)
        tail = pl.ds(cols - TILE, TILE)
        plans = (
            (colsend.at[step, 0], colrecv.at[step, 1], (gi, left)),
            (colsend.at[step, 1], colrecv.at[step, 0], (gi, right)),
            (xpad.at[:, top, pl.ds(0, cols)], rowrecv.at[step, 1], (up, gj)),
            (xpad.at[:, bottom, pl.ds(0, cols)], rowrecv.at[step, 0], (down, gj)),
            (xpad.at[:, bottom, tail], cornrecv.at[step, 0], (down, right)),
            (xpad.at[:, bottom, head], cornrecv.at[step, 1], (down, left)),
            (xpad.at[:, top, tail], cornrecv.at[step, 2], (up, right)),
            (xpad.at[:, top, head], cornrecv.at[step, 3], (up, left)),
        )
        halos = [
            pltpu.make_async_remote_copy(
                src_ref=src, dst_ref=dst, send_sem=halo_send.at[step, i], recv_sem=halo_recv.at[step, i],
                device_id=where, device_id_type=MESH)
            for i, (src, dst, where) in enumerate(plans)
        ]
        for copy in halos:
            copy.start()
        for copy in halos:
            copy.wait()

        joined = jnp.concatenate(
            [colrecv[step, 0], colrecv[step, 1], jnp.zeros((TILE - 16, rows), f32)], axis=0)
        sides = jnp.transpose(joined)
        lane8 = lax.broadcasted_iota(jnp.int32, (8, TILE), 1)
        for c in range(3):
            before = pltpu.roll(sides, 126 - 2 * c, 1) * has_left
            after = pltpu.roll(sides, 120 - 2 * c, 1) * has_right
            xpad[c, 8:8 + rows, cols:wide] = jnp.where(lane < 64, after, before)
            xpad[c, 0:8, 0:cols] = rowrecv[step, 0, c] * has_up
            xpad[c, 8 + rows:16 + rows, 0:cols] = rowrecv[step, 1, c] * has_down
            xpad[c, 0:8, cols:wide] = jnp.where(
                lane8 < 64, cornrecv[step, 1, c] * has_right, cornrecv[step, 0, c] * has_left) * has_up
            xpad[c, 8 + rows:16 + rows, cols:wide] = jnp.where(
                lane8 < 64, cornrecv[step, 3, c] * has_right, cornrecv[step, 2, c] * has_left) * has_down

        tall = CHUNK + 16

        def above(v):
            return pltpu.roll(v, 1, 0)

        def below(v):
            return pltpu.roll(v, tall - 1, 0)

        def before(v):
            return pltpu.roll(v, 1, 1)

        def after(v):
            return pltpu.roll(v, wide - 1, 1)

        def internal(chunk, carry):
            r0 = pl.multiple_of(chunk * CHUNK, CHUNK)
            x = [xpad[c, pl.ds(r0, tall), :] for c in range(3)]
            xa = [after(v) for v in x]
            xb = [below(v) for v in x]
            row = lax.broadcasted_iota(jnp.int32, (tall, wide), 0) + (r0 - 8)
            col = lax.broadcasted_iota(jnp.int32, (tall, wide), 1)
            mask = jnp.where(row < 0, has_up, jnp.where(row >= rows, has_down, 1.0))
            mask = mask * jnp.where(col == cols, has_right, jnp.where(col == wide - 1, has_left, 1.0))
            ea = [p - q for p, q in zip(xa, x)]
            eb = [p - q for p, q in zip(xb, x)]
            ga = 1.0 + hardening * (ea[0] * ea[0] + ea[1] * ea[1] + ea[2] * ea[2])
            gb = 1.0 + hardening * (eb[0] * eb[0] + eb[1] * eb[1] + eb[2] * eb[2])
            stiff = stiff_ref[pl.ds(r0, CHUNK), :]
            for c in range(3):
                fa = ea[c] * ga
                fb = eb[c] * gb
                pull = (fa - before(fa)) + (fb - above(fb))
                curve = ((ea[c] - before(ea[c])) + (eb[c] - above(eb[c]))) * mask
                bend = (above(curve) + below(curve)) + (before(curve) + after(curve)) - 4.0 * curve
                force[c, pl.ds(r0, CHUNK), :] = (
                    stiff * pull[8:8 + CHUNK, 0:cols] - bend_gain * bend[8:8 + CHUNK, 0:cols])
            return carry

        lax.fori_loop(0, rows // CHUNK, internal, 0)

        def tiles_in(d, carry):
            tile_copy(step, me, lax.rem(me + d, n)).wait_recv()
            return carry

        lax.fori_loop(1, n, tiles_in, 0)
        for k in range(slots):
            for c in range(3):
                rec8[k * n:(k + 1) * n, c, :] = recv[step, :, k * 3 + c, :] * SCALE

        def split_slots(g, carry):
            at = pl.ds(g * 8, 8)
            hi, mid, lo = split3(rec8[at])
            second = mid.astype(f32) + pltpu.roll(lo.astype(f32), 4, 1)
            aug[at] = jnp.concatenate([hi.astype(f32), second], axis=1).astype(bf16)
            return carry

        lax.fori_loop(0, total // 8, split_slots, 0)

        def sums(out):
            out = out[0:8] + out[8:16]
            return out + pltpu.roll(out, 4, 0)

        def pairs(g, carry):
            for u in range(UNROLL):
                m = g * UNROLL + u
                a = jnp.maximum(pair_s[0, m], 0)
                b = jnp.maximum(pair_s[1, m], 0)
                p = jnp.transpose(rec8[a])
                q = rec8[b]
                power = jnp.full((TILE, TILE), -2.0, f32)
                for c in range(3):
                    d = p[:, c:c + 1] - q[c:c + 1, :]
                    power = power - d * d
                w = jnp.exp2(power)
                hi = w.astype(bf16)
                lo = (w - hi.astype(f32)).astype(bf16)
                pa = aug[a]
                qb = aug[b]
                pa = jnp.concatenate([pa, pa], axis=1)
                qb = jnp.concatenate([qb, qb], axis=1)
                far = jnp.dot(pa, jnp.concatenate([hi, lo], axis=0), preferred_element_type=f32)
                near = lax.dot_general(
                    qb, jnp.concatenate([hi, lo], axis=1), (((1,), (1,)), ((), ())),
                    preferred_element_type=f32)
                pairsum[m] = sums(near)
                pairsum[number + m] = sums(far)
            return carry

        lax.fori_loop(0, number // UNROLL, pairs, 0)

        ids = lax.broadcasted_iota(jnp.int32, (total, number), 0)
        hot = jnp.concatenate(
            [(ids == pair_v[0:1, :]).astype(f32), (ids == pair_v[1:2, :]).astype(f32)], axis=1).astype(bf16)
        summed = []
        for c in range(4):
            parts = split3(pairsum[:, c, :])
            summed.append(sum(jnp.dot(hot, part, preferred_element_type=f32) for part in parts))
        for c in range(3):
            push = (rec8[:, c, :] * summed[3] - summed[c]) * (1.0 / SCALE)
            for k in range(slots):
                backsend[step, :, k * 3 + c, :] = push[k * n:(k + 1) * n]

        def send_back(d, carry):
            back_copy(step, lax.rem(me + d, n), me).start()
            return carry

        lax.fori_loop(1, n, send_back, 0)
        back[step, me] = backsend[step, me]

        def back_in(d, carry):
            back_copy(step, me, lax.rem(me + d, n)).wait_recv()
            return carry

        lax.fori_loop(1, n, back_in, 0)

        parts = [split3(jnp.concatenate([back[step, :, k * 3 + c, :] for k in range(slots)], axis=0))
                 for c in range(3)]
        parts = [jnp.concatenate([parts[c][i] for c in range(3)], axis=1) for i in range(3)]
        parts = jnp.concatenate(parts, axis=0)

        def advance(chunk, carry):
            r0 = pl.multiple_of(chunk * CHUNK, CHUNK)
            span = pl.ds(r0, CHUNK)
            ids = lax.broadcasted_iota(jnp.int32, (CHUNK, total), 0) + r0
            in_row = ids == route_v[0:1, :]
            for t in range(cols // TILE):
                at = slice(t * TILE, (t + 1) * TILE)
                hot = (in_row & (route_v[1:2, :] == t)).astype(f32).astype(bf16)
                hot = jnp.concatenate([hot, hot, hot], axis=1)
                contact = jnp.dot(hot, parts, preferred_element_type=f32)
                for c in range(3):
                    v = vel_out[c, span, at]
                    push = force[c, span, at] + contact[:, c * TILE:(c + 1) * TILE]
                    v = v + time_step * (push - damping * v)
                    x = xpad[c, pl.ds(r0 + 8, CHUNK), at] + time_step * v
                    vel_out[c, span, at] = v
                    xpad[c, pl.ds(r0 + 8, CHUNK), at] = x
                    blocks[t, c, span, :] = x
                    pos_out[c, span, at] = x
            return carry

        lax.fori_loop(0, rows // CHUNK, advance, 0)

        def sent(d, carry):
            o = lax.rem(me + d, n)
            tile_copy(step, o, me).wait_send()
            back_copy(step, o, me).wait_send()
            return carry

        lax.fori_loop(1, n, sent, 0)
        return carry

    lax.fori_loop(0, STEPS, run_step, 0)


def local(ngx, ngy, positions, velocity, stiffness, send_tiles, pair_tiles):
    n = ngx * ngy
    rows, cols = stiffness.shape
    route = send_tiles.reshape(n, -1).T.reshape(-1)
    slots = route.shape[0] // n
    total = n * slots
    per_row = cols // TILE
    route = jnp.where(route >= 0, jnp.stack([route // per_row, route % per_row]), -1)
    paired = pair_tiles.reshape(2, -1)
    paired = jnp.where(paired >= 0, (paired % slots) * n + paired // slots, -1)
    number = paired.shape[1]
    vmem = pl.BlockSpec(memory_space=pltpu.VMEM)
    smem = pl.BlockSpec(memory_space=pltpu.SMEM)
    dma = pltpu.SemaphoreType.DMA
    shape = jax.ShapeDtypeStruct(positions.shape, f32)
    return pl.pallas_call(
        functools.partial(kernel, ngx, ngy, slots),
        out_shape=(shape, shape),
        in_specs=[vmem, vmem, vmem, smem, vmem, smem, vmem],
        out_specs=(vmem, vmem),
        scratch_shapes=[
            pltpu.VMEM((3, rows + 16, cols + TILE), f32),
            pltpu.VMEM((cols // TILE, 3, rows, TILE), f32),
            pltpu.VMEM((3, rows, cols), f32),
            pltpu.VMEM((STEPS, n, slots * 3, TILE), f32),
            pltpu.VMEM((STEPS, n, slots * 3, TILE), f32),
            pltpu.VMEM((STEPS, n, slots * 3, TILE), f32),
            pltpu.VMEM((STEPS, n, slots * 3, TILE), f32),
            pltpu.VMEM((total, 8, TILE), f32),
            pltpu.VMEM((total, 16, TILE), bf16),
            pltpu.VMEM((2 * number, 8, TILE), f32),
            pltpu.VMEM((STEPS, 2, 8, rows), f32),
            pltpu.VMEM((STEPS, 2, 8, rows), f32),
            pltpu.VMEM((STEPS, 2, 3, 8, cols), f32),
            pltpu.VMEM((STEPS, 4, 3, 8, TILE), f32),
            dma((STEPS, n)), dma((STEPS, n)), dma((STEPS, n)), dma((STEPS, n)),
            dma((STEPS, 8)), dma((STEPS, 8)),
        ],
        compiler_params=pltpu.CompilerParams(
            collective_id=0, has_side_effects=True, vmem_limit_bytes=56 * 1024 * 1024),
        name="shell_steps",
    )(positions, velocity, stiffness, route, route, paired, paired)


def solution(mesh):
    ngx, ngy = mesh.shape["gx"], mesh.shape["gy"]
    return jax.shard_map(
        functools.partial(local, ngx, ngy),
        mesh=mesh,
        in_specs=(
            P(None, "gx", "gy"),
            P(None, "gx", "gy"),
            P("gx", "gy"),
            P("gx", "gy"),
            P("gx", "gy", None, None),
        ),
        out_specs=(P(None, "gx", "gy"), P(None, "gx", "gy")),
        check_vma=False,
    )
```

```python
import functools
import math

import jax
import jax.numpy as jnp
from jax import lax
from jax.experimental import pallas as pl
from jax.experimental.pallas import tpu as pltpu
from jax.sharding import PartitionSpec as P

TILE = 128
STEPS = 2
MESH = pl.DeviceIdType.MESH

time_step = 0.1
damping = 0.2
hardening = 0.1
bend_gain = 0.02
SCALE = math.sqrt(0.5 * math.log2(math.e))
CHUNK = 64
UNROLL = 16
bf16 = jnp.bfloat16
f32 = jnp.float32


def split3(x):
    hi = x.astype(bf16)
    rest = x - hi.astype(f32)
    mid = rest.astype(bf16)
    lo = (rest - mid.astype(f32)).astype(bf16)
    return hi, mid, lo


def kernel(ngx, ngy, slots, pos_ref, vel_ref, stiff_ref, route_s, route_v, pair_s, pair_v,
           pos_out, vel_out, xpad, blocks, force, sendbuf, recv, backsend, back, rec8, aug, pairsum,
           colsend, colrecv, rowrecv, cornrecv,
           tile_send, tile_recv, back_send, back_recv, halo_send, halo_recv):
    n = ngx * ngy
    rows, cols = pos_ref.shape[1], pos_ref.shape[2]
    wide = cols + TILE
    number = pair_s.shape[1]
    total = n * slots
    gi = lax.axis_index("gx")
    gj = lax.axis_index("gy")
    me = gi * ngy + gj

    def place(o):
        return (o // ngy, lax.rem(o, ngy))

    barrier = pltpu.get_barrier_semaphore()

    def greet(d, carry):
        pl.semaphore_signal(barrier, inc=1, device_id=place(lax.rem(me + d, n)), device_id_type=MESH)
        return carry

    lax.fori_loop(1, n, greet, 0)

    for c in range(3):
        xpad[c, 8:8 + rows, 0:cols] = pos_ref[c]
        for t in range(cols // TILE):
            blocks[t, c] = pos_ref[c, :, t * TILE:(t + 1) * TILE]
    vel_out[...] = vel_ref[...]
    rec8[...] = jnp.zeros_like(rec8)
    rec8[:, 3, :] = jnp.ones((total, TILE), f32)

    pl.semaphore_wait(barrier, n - 1)

    up = lax.rem(gi + ngx - 1, ngx)
    down = lax.rem(gi + 1, ngx)
    left = lax.rem(gj + ngy - 1, ngy)
    right = lax.rem(gj + 1, ngy)
    has_up = (gi > 0).astype(f32)
    has_down = (gi < ngx - 1).astype(f32)
    has_left = (gj > 0).astype(f32)
    has_right = (gj < ngy - 1).astype(f32)

    def tile_copy(step, o, source):
        return pltpu.make_async_remote_copy(
            src_ref=sendbuf.at[step, o], dst_ref=recv.at[step, source],
            send_sem=tile_send.at[step, o], recv_sem=tile_recv.at[step, source],
            device_id=place(o), device_id_type=MESH)

    def back_copy(step, o, source):
        return pltpu.make_async_remote_copy(
            src_ref=backsend.at[step, o], dst_ref=back.at[step, source],
            send_sem=back_send.at[step, o], recv_sem=back_recv.at[step, source],
            device_id=place(o), device_id_type=MESH)

    def run_step(step, carry):
        def fetch(o, put):
            for k in range(slots):
                at = k * n + o
                row = route_s[0, at]
                col = route_s[1, at]
                filled = (row >= 0).astype(f32)
                row = jnp.maximum(row, 0)
                col = jnp.maximum(col, 0)
                for c in range(3):
                    put(k * 3 + c, blocks[col, c, pl.ds(row, 1), :] * filled)

        top = pl.ds(8, 8)
        bottom = pl.ds(rows, 8)
        head = pl.ds(0, TILE)
        tail = pl.ds(cols - TILE, TILE)
        plans = (
            (colsend.at[step, 0], colrecv.at[step, 1], (gi, left)),
            (colsend.at[step, 1], colrecv.at[step, 0], (gi, right)),
            (xpad.at[:, top, pl.ds(0, cols)], rowrecv.at[step, 1], (up, gj)),
            (xpad.at[:, bottom, pl.ds(0, cols)], rowrecv.at[step, 0], (down, gj)),
            (xpad.at[:, bottom, tail], cornrecv.at[step, 0], (down, right)),
            (xpad.at[:, bottom, head], cornrecv.at[step, 1], (down, left)),
            (xpad.at[:, top, tail], cornrecv.at[step, 2], (up, right)),
            (xpad.at[:, top, head], cornrecv.at[step, 3], (up, left)),
        )
        halos = [
            pltpu.make_async_remote_copy(
                src_ref=src, dst_ref=dst, send_sem=halo_send.at[step, i], recv_sem=halo_recv.at[step, i],
                device_id=where, device_id_type=MESH)
            for i, (src, dst, where) in enumerate(plans)
        ]
        for copy in halos[2:]:
            copy.start()

        def send_tiles(d, carry):
            o = lax.rem(me + d, n)

            def put(j, value):
                sendbuf[step, o, pl.ds(j, 1), :] = value

            fetch(o, put)
            tile_copy(step, o, me).start()
            return carry

        lax.fori_loop(1, n, send_tiles, 0)

        def put_own(j, value):
            recv[step, me, pl.ds(j, 1), :] = value

        fetch(me, put_own)

        lane = lax.broadcasted_iota(jnp.int32, (rows, TILE), 1)
        packed = jnp.zeros((rows, TILE), f32)
        for c in range(3):
            first = pltpu.roll(xpad[c, 8:8 + rows, 0:TILE], 2 * c, 1) if c else xpad[c, 8:8 + rows, 0:TILE]
            last = pltpu.roll(xpad[c, 8:8 + rows, cols - TILE:cols], 10 + 2 * c, 1)
            packed = jnp.where((lane == 2 * c) | (lane == 2 * c + 1), first, packed)
            packed = jnp.where((lane == 8 + 2 * c) | (lane == 9 + 2 * c), last, packed)
        turned = jnp.transpose(packed)
        colsend[step, 0] = turned[0:8]
        colsend[step, 1] = turned[8:16]

        for copy in halos[:2]:
            copy.start()
        for copy in halos:
            copy.wait()

        joined = jnp.concatenate(
            [colrecv[step, 0], colrecv[step, 1], jnp.zeros((TILE - 16, rows), f32)], axis=0)
        sides = jnp.transpose(joined)
        lane8 = lax.broadcasted_iota(jnp.int32, (8, TILE), 1)
        for c in range(3):
            before = pltpu.roll(sides, 126 - 2 * c, 1) * has_left
            after = pltpu.roll(sides, 120 - 2 * c, 1) * has_right
            xpad[c, 8:8 + rows, cols:wide] = jnp.where(lane < 64, after, before)
            xpad[c, 0:8, 0:cols] = rowrecv[step, 0, c] * has_up
            xpad[c, 8 + rows:16 + rows, 0:cols] = rowrecv[step, 1, c] * has_down
            xpad[c, 0:8, cols:wide] = jnp.where(
                lane8 < 64, cornrecv[step, 1, c] * has_right, cornrecv[step, 0, c] * has_left) * has_up
            xpad[c, 8 + rows:16 + rows, cols:wide] = jnp.where(
                lane8 < 64, cornrecv[step, 3, c] * has_right, cornrecv[step, 2, c] * has_left) * has_down

        tall = CHUNK + 16

        def above(v):
            return pltpu.roll(v, 1, 0)

        def below(v):
            return pltpu.roll(v, tall - 1, 0)

        def before(v):
            return pltpu.roll(v, 1, 1)

        def after(v):
            return pltpu.roll(v, wide - 1, 1)

        def internal(chunk, carry):
            r0 = pl.multiple_of(chunk * CHUNK, CHUNK)
            x = [xpad[c, pl.ds(r0, tall), :] for c in range(3)]
            xa = [after(v) for v in x]
            xb = [below(v) for v in x]
            row = lax.broadcasted_iota(jnp.int32, (tall, wide), 0) + (r0 - 8)
            col = lax.broadcasted_iota(jnp.int32, (tall, wide), 1)
            mask = jnp.where(row < 0, has_up, jnp.where(row >= rows, has_down, 1.0))
            mask = mask * jnp.where(col == cols, has_right, jnp.where(col == wide - 1, has_left, 1.0))
            ea = [p - q for p, q in zip(xa, x)]
            eb = [p - q for p, q in zip(xb, x)]
            ga = 1.0 + hardening * (ea[0] * ea[0] + ea[1] * ea[1] + ea[2] * ea[2])
            gb = 1.0 + hardening * (eb[0] * eb[0] + eb[1] * eb[1] + eb[2] * eb[2])
            stiff = stiff_ref[pl.ds(r0, CHUNK), :]
            for c in range(3):
                fa = ea[c] * ga
                fb = eb[c] * gb
                pull = (fa - before(fa)) + (fb - above(fb))
                curve = ((ea[c] - before(ea[c])) + (eb[c] - above(eb[c]))) * mask
                bend = (above(curve) + below(curve)) + (before(curve) + after(curve)) - 4.0 * curve
                force[c, pl.ds(r0, CHUNK), :] = (
                    stiff * pull[8:8 + CHUNK, 0:cols] - bend_gain * bend[8:8 + CHUNK, 0:cols])
            return carry

        half = rows // CHUNK // 2
        lax.fori_loop(0, half, internal, 0)

        def tiles_in(d, carry):
            tile_copy(step, me, lax.rem(me + d, n)).wait_recv()
            return carry

        lax.fori_loop(1, n, tiles_in, 0)
        for k in range(slots):
            for c in range(3):
                rec8[k * n:(k + 1) * n, c, :] = recv[step, :, k * 3 + c, :] * SCALE

        def split_slots(g, carry):
            at = pl.ds(g * 8, 8)
            hi, mid, lo = split3(rec8[at])
            second = mid.astype(f32) + pltpu.roll(lo.astype(f32), 4, 1)
            aug[at] = jnp.concatenate([hi.astype(f32), second], axis=1).astype(bf16)
            return carry

        lax.fori_loop(0, total // 8, split_slots, 0)

        def sums(out):
            out = out[0:8] + out[8:16]
            return out + pltpu.roll(out, 4, 0)

        def slot_row(s):
            return lax.rem(s, slots) * n + lax.div(s, slots)

        def pairs(g, carry):
            for u in range(UNROLL):
                m = g * UNROLL + u
                a = slot_row(jnp.maximum(pair_s[0, m], 0))
                b = slot_row(jnp.maximum(pair_s[1, m], 0))
                p = jnp.transpose(rec8[a])
                q = rec8[b]
                power = jnp.full((TILE, TILE), -2.0, f32)
                for c in range(3):
                    d = p[:, c:c + 1] - q[c:c + 1, :]
                    power = power - d * d
                w = jnp.exp2(power)
                hi = w.astype(bf16)
                lo = (w - hi.astype(f32)).astype(bf16)
                pa = aug[a]
                qb = aug[b]
                pa = jnp.concatenate([pa, pa], axis=1)
                qb = jnp.concatenate([qb, qb], axis=1)
                far = jnp.dot(pa, jnp.concatenate([hi, lo], axis=0), preferred_element_type=f32)
                near = lax.dot_general(
                    qb, jnp.concatenate([hi, lo], axis=1), (((1,), (1,)), ((), ())),
                    preferred_element_type=f32)
                pairsum[m] = sums(near)
                pairsum[number + m] = sums(far)
            return carry

        lax.fori_loop(0, number // UNROLL, pairs, 0)

        ids = lax.broadcasted_iota(jnp.int32, (total, number), 0)
        ids = lax.rem(ids, n) * slots + lax.div(ids, n)
        hot = jnp.concatenate(
            [(ids == pair_v[0:1, :]).astype(f32), (ids == pair_v[1:2, :]).astype(f32)], axis=1).astype(bf16)
        summed = []
        for c in range(4):
            parts = split3(pairsum[:, c, :])
            summed.append(sum(jnp.dot(hot, part, preferred_element_type=f32) for part in parts))
        for c in range(3):
            push = (rec8[:, c, :] * summed[3] - summed[c]) * (1.0 / SCALE)
            for k in range(slots):
                backsend[step, :, k * 3 + c, :] = push[k * n:(k + 1) * n]

        def send_back(d, carry):
            back_copy(step, lax.rem(me + d, n), me).start()
            return carry

        lax.fori_loop(1, n, send_back, 0)
        back[step, me] = backsend[step, me]
        lax.fori_loop(half, rows // CHUNK, internal, 0)

        def back_in(d, carry):
            back_copy(step, me, lax.rem(me + d, n)).wait_recv()
            return carry

        lax.fori_loop(1, n, back_in, 0)

        parts = [split3(jnp.concatenate([back[step, :, k * 3 + c, :] for k in range(slots)], axis=0))
                 for c in range(3)]
        parts = [jnp.concatenate([parts[c][i] for c in range(3)], axis=1) for i in range(3)]
        parts = jnp.concatenate(parts, axis=0)

        in_row = lax.broadcasted_iota(jnp.int32, (rows, total), 0) == route_v[0:1, :]
        for t in range(cols // TILE):
            at = slice(t * TILE, (t + 1) * TILE)
            hot = (in_row & (route_v[1:2, :] == t)).astype(f32).astype(bf16)
            hot = jnp.concatenate([hot, hot, hot], axis=1)
            contact = jnp.dot(hot, parts, preferred_element_type=f32)
            for c in range(3):
                v = vel_out[c, :, at]
                push = force[c, :, at] + contact[:, c * TILE:(c + 1) * TILE]
                v = v + time_step * (push - damping * v)
                x = xpad[c, 8:8 + rows, at] + time_step * v
                vel_out[c, :, at] = v
                xpad[c, 8:8 + rows, at] = x
                blocks[t, c] = x
                pos_out[c, :, at] = x

        def sent(d, carry):
            o = lax.rem(me + d, n)
            tile_copy(step, o, me).wait_send()
            back_copy(step, o, me).wait_send()
            return carry

        lax.fori_loop(1, n, sent, 0)
        return carry

    lax.fori_loop(0, STEPS, run_step, 0)


def local(ngx, ngy, positions, velocity, stiffness, send_tiles, pair_tiles):
    n = ngx * ngy
    rows, cols = stiffness.shape
    route = send_tiles.reshape(n, -1).T.reshape(-1)
    slots = route.shape[0] // n
    total = n * slots
    per_row = cols // TILE
    route = jnp.where(route >= 0, jnp.stack([route // per_row, route % per_row]), -1)
    paired = pair_tiles.reshape(2, -1)
    number = paired.shape[1]
    vmem = pl.BlockSpec(memory_space=pltpu.VMEM)
    smem = pl.BlockSpec(memory_space=pltpu.SMEM)
    dma = pltpu.SemaphoreType.DMA
    shape = jax.ShapeDtypeStruct(positions.shape, f32)
    return pl.pallas_call(
        functools.partial(kernel, ngx, ngy, slots),
        out_shape=(shape, shape),
        in_specs=[vmem, vmem, vmem, smem, vmem, smem, vmem],
        out_specs=(vmem, vmem),
        scratch_shapes=[
            pltpu.VMEM((3, rows + 16, cols + TILE), f32),
            pltpu.VMEM((cols // TILE, 3, rows, TILE), f32),
            pltpu.VMEM((3, rows, cols), f32),
            pltpu.VMEM((STEPS, n, slots * 3, TILE), f32),
            pltpu.VMEM((STEPS, n, slots * 3, TILE), f32),
            pltpu.VMEM((STEPS, n, slots * 3, TILE), f32),
            pltpu.VMEM((STEPS, n, slots * 3, TILE), f32),
            pltpu.VMEM((total, 8, TILE), f32),
            pltpu.VMEM((total, 16, TILE), bf16),
            pltpu.VMEM((2 * number, 8, TILE), f32),
            pltpu.VMEM((STEPS, 2, 8, rows), f32),
            pltpu.VMEM((STEPS, 2, 8, rows), f32),
            pltpu.VMEM((STEPS, 2, 3, 8, cols), f32),
            pltpu.VMEM((STEPS, 4, 3, 8, TILE), f32),
            dma((STEPS, n)), dma((STEPS, n)), dma((STEPS, n)), dma((STEPS, n)),
            dma((STEPS, 8)), dma((STEPS, 8)),
        ],
        compiler_params=pltpu.CompilerParams(
            collective_id=0, has_side_effects=True, vmem_limit_bytes=56 * 1024 * 1024),
        name="shell_steps",
    )(positions, velocity, stiffness, route, route, paired, paired)


def solution(mesh):
    ngx, ngy = mesh.shape["gx"], mesh.shape["gy"]
    return jax.shard_map(
        functools.partial(local, ngx, ngy),
        mesh=mesh,
        in_specs=(
            P(None, "gx", "gy"),
            P(None, "gx", "gy"),
            P("gx", "gy"),
            P("gx", "gy"),
            P("gx", "gy", None, None),
        ),
        out_specs=(P(None, "gx", "gy"), P(None, "gx", "gy")),
        check_vma=False,
    )
```

```python
import functools
import math

import jax
import jax.numpy as jnp
from jax import lax
from jax.experimental import pallas as pl
from jax.experimental.pallas import tpu as pltpu
from jax.sharding import PartitionSpec as P

TILE = 128
STEPS = 2
MESH = pl.DeviceIdType.MESH

time_step = 0.1
damping = 0.2
hardening = 0.1
bend_gain = 0.02
SCALE = math.sqrt(0.5 * math.log2(math.e))
CHUNK = 64
UNROLL = 16
bf16 = jnp.bfloat16
f32 = jnp.float32


def split3(x):
    hi = x.astype(bf16)
    rest = x - hi.astype(f32)
    mid = rest.astype(bf16)
    lo = (rest - mid.astype(f32)).astype(bf16)
    return hi, mid, lo


def kernel(ngx, ngy, slots, pos_ref, vel_ref, stiff_ref, route_s, route_v, pair_s, pair_v,
           pos_out, vel_out, xpad, blocks, force, sendbuf, recv, backsend, back, rec8, aug, left_side, right_side, pairsum,
           colsend, colrecv, rowrecv, cornrecv,
           tile_send, tile_recv, back_send, back_recv, halo_send, halo_recv):
    n = ngx * ngy
    rows, cols = pos_ref.shape[1], pos_ref.shape[2]
    wide = cols + TILE
    number = pair_s.shape[1]
    total = n * slots
    gi = lax.axis_index("gx")
    gj = lax.axis_index("gy")
    me = gi * ngy + gj

    def place(o):
        return (o // ngy, lax.rem(o, ngy))

    barrier = pltpu.get_barrier_semaphore()

    def greet(d, carry):
        pl.semaphore_signal(barrier, inc=1, device_id=place(lax.rem(me + d, n)), device_id_type=MESH)
        return carry

    lax.fori_loop(1, n, greet, 0)

    for c in range(3):
        xpad[c, 8:8 + rows, 0:cols] = pos_ref[c]
        for t in range(cols // TILE):
            blocks[t, c] = pos_ref[c, :, t * TILE:(t + 1) * TILE]
    vel_out[...] = vel_ref[...]
    rec8[...] = jnp.zeros_like(rec8)
    rec8[:, 3, :] = jnp.ones((total, TILE), f32)

    pl.semaphore_wait(barrier, n - 1)

    up = lax.rem(gi + ngx - 1, ngx)
    down = lax.rem(gi + 1, ngx)
    left = lax.rem(gj + ngy - 1, ngy)
    right = lax.rem(gj + 1, ngy)
    has_up = (gi > 0).astype(f32)
    has_down = (gi < ngx - 1).astype(f32)
    has_left = (gj > 0).astype(f32)
    has_right = (gj < ngy - 1).astype(f32)

    def tile_copy(step, o, source):
        return pltpu.make_async_remote_copy(
            src_ref=sendbuf.at[o], dst_ref=recv.at[step, source],
            send_sem=tile_send.at[step, o], recv_sem=tile_recv.at[step, source],
            device_id=place(o), device_id_type=MESH)

    def back_copy(step, o, source):
        return pltpu.make_async_remote_copy(
            src_ref=backsend.at[o], dst_ref=back.at[step, source],
            send_sem=back_send.at[step, o], recv_sem=back_recv.at[step, source],
            device_id=place(o), device_id_type=MESH)

    def run_step(step, carry):
        def fetch(o, put):
            for k in range(slots):
                at = k * n + o
                row = route_s[0, at]
                col = route_s[1, at]
                filled = (row >= 0).astype(f32)
                row = jnp.maximum(row, 0)
                col = jnp.maximum(col, 0)
                for c in range(3):
                    put(k * 3 + c, blocks[col, c, pl.ds(row, 1), :] * filled)

        top = pl.ds(8, 8)
        bottom = pl.ds(rows, 8)
        head = pl.ds(0, TILE)
        tail = pl.ds(cols - TILE, TILE)
        plans = (
            (colsend.at[step, 0], colrecv.at[step, 1], (gi, left)),
            (colsend.at[step, 1], colrecv.at[step, 0], (gi, right)),
            (xpad.at[:, top, pl.ds(0, cols)], rowrecv.at[step, 1], (up, gj)),
            (xpad.at[:, bottom, pl.ds(0, cols)], rowrecv.at[step, 0], (down, gj)),
            (xpad.at[:, bottom, tail], cornrecv.at[step, 0], (down, right)),
            (xpad.at[:, bottom, head], cornrecv.at[step, 1], (down, left)),
            (xpad.at[:, top, tail], cornrecv.at[step, 2], (up, right)),
            (xpad.at[:, top, head], cornrecv.at[step, 3], (up, left)),
        )
        halos = [
            pltpu.make_async_remote_copy(
                src_ref=src, dst_ref=dst, send_sem=halo_send.at[step, i], recv_sem=halo_recv.at[step, i],
                device_id=where, device_id_type=MESH)
            for i, (src, dst, where) in enumerate(plans)
        ]
        for copy in halos[2:]:
            copy.start()

        def send_tiles(d, carry):
            o = lax.rem(me + d, n)

            def put(j, value):
                sendbuf[o, pl.ds(j, 1), :] = value

            fetch(o, put)
            tile_copy(step, o, me).start()
            return carry

        lax.fori_loop(1, n, send_tiles, 0)

        def put_own(j, value):
            recv[step, me, pl.ds(j, 1), :] = value

        fetch(me, put_own)

        lane = lax.broadcasted_iota(jnp.int32, (rows, TILE), 1)
        packed = jnp.zeros((rows, TILE), f32)
        for c in range(3):
            first = pltpu.roll(xpad[c, 8:8 + rows, 0:TILE], 2 * c, 1) if c else xpad[c, 8:8 + rows, 0:TILE]
            last = pltpu.roll(xpad[c, 8:8 + rows, cols - TILE:cols], 10 + 2 * c, 1)
            packed = jnp.where((lane == 2 * c) | (lane == 2 * c + 1), first, packed)
            packed = jnp.where((lane == 8 + 2 * c) | (lane == 9 + 2 * c), last, packed)
        turned = jnp.transpose(packed)
        colsend[step, 0] = turned[0:8]
        colsend[step, 1] = turned[8:16]

        for copy in halos[:2]:
            copy.start()
        for copy in halos:
            copy.wait()

        joined = jnp.concatenate(
            [colrecv[step, 0], colrecv[step, 1], jnp.zeros((TILE - 16, rows), f32)], axis=0)
        sides = jnp.transpose(joined)
        lane8 = lax.broadcasted_iota(jnp.int32, (8, TILE), 1)
        for c in range(3):
            before = pltpu.roll(sides, 126 - 2 * c, 1) * has_left
            after = pltpu.roll(sides, 120 - 2 * c, 1) * has_right
            xpad[c, 8:8 + rows, cols:wide] = jnp.where(lane < 64, after, before)
            xpad[c, 0:8, 0:cols] = rowrecv[step, 0, c] * has_up
            xpad[c, 8 + rows:16 + rows, 0:cols] = rowrecv[step, 1, c] * has_down
            xpad[c, 0:8, cols:wide] = jnp.where(
                lane8 < 64, cornrecv[step, 1, c] * has_right, cornrecv[step, 0, c] * has_left) * has_up
            xpad[c, 8 + rows:16 + rows, cols:wide] = jnp.where(
                lane8 < 64, cornrecv[step, 3, c] * has_right, cornrecv[step, 2, c] * has_left) * has_down

        tall = CHUNK + 16

        def above(v):
            return pltpu.roll(v, 1, 0)

        def below(v):
            return pltpu.roll(v, tall - 1, 0)

        def before(v):
            return pltpu.roll(v, 1, 1)

        def after(v):
            return pltpu.roll(v, wide - 1, 1)

        def internal(chunk, carry):
            r0 = pl.multiple_of(chunk * CHUNK, CHUNK)
            x = [xpad[c, pl.ds(r0, tall), :] for c in range(3)]
            xa = [after(v) for v in x]
            xb = [below(v) for v in x]
            row = lax.broadcasted_iota(jnp.int32, (tall, wide), 0) + (r0 - 8)
            col = lax.broadcasted_iota(jnp.int32, (tall, wide), 1)
            mask = jnp.where(row < 0, has_up, jnp.where(row >= rows, has_down, 1.0))
            mask = mask * jnp.where(col == cols, has_right, jnp.where(col == wide - 1, has_left, 1.0))
            ea = [p - q for p, q in zip(xa, x)]
            eb = [p - q for p, q in zip(xb, x)]
            ga = 1.0 + hardening * (ea[0] * ea[0] + ea[1] * ea[1] + ea[2] * ea[2])
            gb = 1.0 + hardening * (eb[0] * eb[0] + eb[1] * eb[1] + eb[2] * eb[2])
            stiff = stiff_ref[pl.ds(r0, CHUNK), :]
            for c in range(3):
                fa = ea[c] * ga
                fb = eb[c] * gb
                pull = (fa - before(fa)) + (fb - above(fb))
                curve = ((ea[c] - before(ea[c])) + (eb[c] - above(eb[c]))) * mask
                bend = (above(curve) + below(curve)) + (before(curve) + after(curve)) - 4.0 * curve
                force[c, pl.ds(r0, CHUNK), :] = (
                    stiff * pull[8:8 + CHUNK, 0:cols] - bend_gain * bend[8:8 + CHUNK, 0:cols])
            return carry

        half = rows // CHUNK // 2
        lax.fori_loop(0, half, internal, 0)

        def tiles_in(d, carry):
            tile_copy(step, me, lax.rem(me + d, n)).wait_recv()
            return carry

        lax.fori_loop(1, n, tiles_in, 0)
        for k in range(slots):
            for c in range(3):
                rec8[k * n:(k + 1) * n, c, :] = recv[step, :, k * 3 + c, :] * SCALE

        def split_slots(g, carry):
            at = pl.ds(g * 8, 8)
            x = rec8[at]
            hi, mid, lo = [part.astype(f32) for part in split3(x)]
            second = mid + pltpu.roll(lo, 4, 1)
            aug[at] = jnp.concatenate([hi, second], axis=1).astype(bf16)
            norm = -1.0 - jnp.sum(x * x, axis=1, keepdims=True)
            nh, nm, nl = [part.astype(f32) for part in split3(norm)]
            row = lax.broadcasted_iota(jnp.int32, x.shape, 1)
            zero = jnp.zeros_like(x)
            ones = jnp.where(row < 6, 1.0, zero)
            own = jnp.where(row == 0, nh, jnp.where(row == 1, nm, jnp.where(row == 2, nl, ones)))
            other = jnp.where(row == 3, nh, jnp.where(row == 4, nm, jnp.where(row == 5, nl, ones)))
            hi2, mid2, lo2 = 2.0 * hi, 2.0 * mid, 2.0 * lo

            def both(upper, lower):
                return upper + pltpu.roll(lower, 4, 1)

            right_side[at] = jnp.concatenate(
                [both(hi2, mid2), both(hi2, lo2), both(hi2, mid2), other], axis=1).astype(bf16)
            whole = jnp.concatenate([both(hi, hi), both(mid, hi), both(lo, mid), own], axis=1)
            for i in range(8):
                left_side[g * 8 + i] = jnp.transpose(whole[i]).astype(bf16)
            return carry

        lax.fori_loop(0, total // 8, split_slots, 0)

        def sums(out):
            out = out[0:8] + out[8:16]
            return out + pltpu.roll(out, 4, 0)

        def slot_row(s):
            return lax.rem(s, slots) * n + lax.div(s, slots)

        def pairs(g, carry):
            for u in range(UNROLL):
                m = g * UNROLL + u
                a = slot_row(jnp.maximum(pair_s[0, m], 0))
                b = slot_row(jnp.maximum(pair_s[1, m], 0))
                power = jnp.dot(left_side[a], right_side[b], preferred_element_type=f32)
                w = jnp.exp2(power)
                hi = w.astype(bf16)
                lo = (w - hi.astype(f32)).astype(bf16)
                pa = aug[a]
                qb = aug[b]
                pa = jnp.concatenate([pa, pa], axis=1)
                qb = jnp.concatenate([qb, qb], axis=1)
                far = jnp.dot(pa, jnp.concatenate([hi, lo], axis=0), preferred_element_type=f32)
                near = lax.dot_general(
                    qb, jnp.concatenate([hi, lo], axis=1), (((1,), (1,)), ((), ())),
                    preferred_element_type=f32)
                pairsum[m] = sums(near)
                pairsum[number + m] = sums(far)
            return carry

        lax.fori_loop(0, number // UNROLL, pairs, 0)

        ids = lax.broadcasted_iota(jnp.int32, (total, number), 0)
        ids = lax.rem(ids, n) * slots + lax.div(ids, n)
        hot = jnp.concatenate(
            [(ids == pair_v[0:1, :]).astype(f32), (ids == pair_v[1:2, :]).astype(f32)], axis=1).astype(bf16)
        summed = []
        for c in range(4):
            parts = split3(pairsum[:, c, :])
            summed.append(sum(jnp.dot(hot, part, preferred_element_type=f32) for part in parts))
        for c in range(3):
            push = (rec8[:, c, :] * summed[3] - summed[c]) * (1.0 / SCALE)
            for k in range(slots):
                backsend[:, k * 3 + c, :] = push[k * n:(k + 1) * n]

        def send_back(d, carry):
            back_copy(step, lax.rem(me + d, n), me).start()
            return carry

        lax.fori_loop(1, n, send_back, 0)
        back[step, me] = backsend[me]
        lax.fori_loop(half, rows // CHUNK, internal, 0)

        def back_in(d, carry):
            back_copy(step, me, lax.rem(me + d, n)).wait_recv()
            return carry

        lax.fori_loop(1, n, back_in, 0)

        parts = [split3(jnp.concatenate([back[step, :, k * 3 + c, :] for k in range(slots)], axis=0))
                 for c in range(3)]
        parts = [jnp.concatenate([parts[c][i] for c in range(3)], axis=1) for i in range(3)]
        parts = jnp.concatenate(parts, axis=0)

        in_row = lax.broadcasted_iota(jnp.int32, (rows, total), 0) == route_v[0:1, :]
        for t in range(cols // TILE):
            at = slice(t * TILE, (t + 1) * TILE)
            hot = (in_row & (route_v[1:2, :] == t)).astype(f32).astype(bf16)
            hot = jnp.concatenate([hot, hot, hot], axis=1)
            contact = jnp.dot(hot, parts, preferred_element_type=f32)
            for c in range(3):
                v = vel_out[c, :, at]
                push = force[c, :, at] + contact[:, c * TILE:(c + 1) * TILE]
                v = v + time_step * (push - damping * v)
                x = xpad[c, 8:8 + rows, at] + time_step * v
                vel_out[c, :, at] = v
                xpad[c, 8:8 + rows, at] = x
                blocks[t, c] = x
                pos_out[c, :, at] = x

        def sent(d, carry):
            o = lax.rem(me + d, n)
            tile_copy(step, o, me).wait_send()
            back_copy(step, o, me).wait_send()
            return carry

        lax.fori_loop(1, n, sent, 0)
        return carry

    lax.fori_loop(0, STEPS, run_step, 0)


def local(ngx, ngy, positions, velocity, stiffness, send_tiles, pair_tiles):
    n = ngx * ngy
    rows, cols = stiffness.shape
    route = send_tiles.reshape(n, -1).T.reshape(-1)
    slots = route.shape[0] // n
    total = n * slots
    per_row = cols // TILE
    route = jnp.where(route >= 0, jnp.stack([route // per_row, route % per_row]), -1)
    paired = pair_tiles.reshape(2, -1)
    number = paired.shape[1]
    vmem = pl.BlockSpec(memory_space=pltpu.VMEM)
    smem = pl.BlockSpec(memory_space=pltpu.SMEM)
    dma = pltpu.SemaphoreType.DMA
    shape = jax.ShapeDtypeStruct(positions.shape, f32)
    return pl.pallas_call(
        functools.partial(kernel, ngx, ngy, slots),
        out_shape=(shape, shape),
        in_specs=[vmem, vmem, vmem, smem, vmem, smem, vmem],
        out_specs=(vmem, vmem),
        scratch_shapes=[
            pltpu.VMEM((3, rows + 16, cols + TILE), f32),
            pltpu.VMEM((cols // TILE, 3, rows, TILE), f32),
            pltpu.VMEM((3, rows, cols), f32),
            pltpu.VMEM((n, slots * 3, TILE), f32),
            pltpu.VMEM((STEPS, n, slots * 3, TILE), f32),
            pltpu.VMEM((n, slots * 3, TILE), f32),
            pltpu.VMEM((STEPS, n, slots * 3, TILE), f32),
            pltpu.VMEM((total, 8, TILE), f32),
            pltpu.VMEM((total, 16, TILE), bf16),
            pltpu.VMEM((total, TILE, 32), bf16),
            pltpu.VMEM((total, 32, TILE), bf16),
            pltpu.VMEM((2 * number, 8, TILE), f32),
            pltpu.VMEM((STEPS, 2, 8, rows), f32),
            pltpu.VMEM((STEPS, 2, 8, rows), f32),
            pltpu.VMEM((STEPS, 2, 3, 8, cols), f32),
            pltpu.VMEM((STEPS, 4, 3, 8, TILE), f32),
            dma((STEPS, n)), dma((STEPS, n)), dma((STEPS, n)), dma((STEPS, n)),
            dma((STEPS, 8)), dma((STEPS, 8)),
        ],
        compiler_params=pltpu.CompilerParams(
            collective_id=0, has_side_effects=True, vmem_limit_bytes=60 * 1024 * 1024),
        name="shell_steps",
    )(positions, velocity, stiffness, route, route, paired, paired)


def solution(mesh):
    ngx, ngy = mesh.shape["gx"], mesh.shape["gy"]
    return jax.shard_map(
        functools.partial(local, ngx, ngy),
        mesh=mesh,
        in_specs=(
            P(None, "gx", "gy"),
            P(None, "gx", "gy"),
            P("gx", "gy"),
            P("gx", "gy"),
            P("gx", "gy", None, None),
        ),
        out_specs=(P(None, "gx", "gy"), P(None, "gx", "gy")),
        check_vma=False,
    )
```

```python
import functools
import math

import jax
import jax.numpy as jnp
from jax import lax
from jax.experimental import pallas as pl
from jax.experimental.pallas import tpu as pltpu
from jax.sharding import PartitionSpec as P

TILE = 128
STEPS = 2
MESH = pl.DeviceIdType.MESH

time_step = 0.1
damping = 0.2
hardening = 0.1
bend_gain = 0.02
SCALE = math.sqrt(0.5 * math.log2(math.e))
CHUNK = 64
UNROLL = 16
BLOCK = 32
bf16 = jnp.bfloat16
f32 = jnp.float32


def split3(x):
    hi = x.astype(bf16)
    rest = x - hi.astype(f32)
    mid = rest.astype(bf16)
    lo = (rest - mid.astype(f32)).astype(bf16)
    return hi, mid, lo


def kernel(ngx, ngy, slots, pos_ref, vel_ref, stiff_ref, route_s, route_v, pair_s, pair_v,
           pos_out, vel_out, xpad, blocks, force, sendbuf, recv, backsend, back, rec8, aug, pairsum,
           colsend, colrecv, rowrecv, cornrecv,
           tile_send, tile_recv, back_send, back_recv, halo_send, halo_recv):
    n = ngx * ngy
    rows, cols = pos_ref.shape[1], pos_ref.shape[2]
    wide = cols + TILE
    number = pair_s.shape[1]
    total = n * slots
    gi = lax.axis_index("gx")
    gj = lax.axis_index("gy")
    me = gi * ngy + gj

    def place(o):
        return (o // ngy, lax.rem(o, ngy))

    barrier = pltpu.get_barrier_semaphore()

    def greet(d, carry):
        pl.semaphore_signal(barrier, inc=1, device_id=place(lax.rem(me + d, n)), device_id_type=MESH)
        return carry

    lax.fori_loop(1, n, greet, 0)

    for c in range(3):
        xpad[c, 8:8 + rows, 0:cols] = pos_ref[c]
        for t in range(cols // TILE):
            blocks[t, c] = pos_ref[c, :, t * TILE:(t + 1) * TILE]
    vel_out[...] = vel_ref[...]
    rec8[...] = jnp.zeros_like(rec8)
    rec8[:, 3, :] = jnp.ones((total, TILE), f32)
    pairsum[number:2 * number] = jnp.zeros((number, 8, TILE), f32)

    pl.semaphore_wait(barrier, n - 1)

    up = lax.rem(gi + ngx - 1, ngx)
    down = lax.rem(gi + 1, ngx)
    left = lax.rem(gj + ngy - 1, ngy)
    right = lax.rem(gj + 1, ngy)
    has_up = (gi > 0).astype(f32)
    has_down = (gi < ngx - 1).astype(f32)
    has_left = (gj > 0).astype(f32)
    has_right = (gj < ngy - 1).astype(f32)

    def tile_copy(step, o, source):
        return pltpu.make_async_remote_copy(
            src_ref=sendbuf.at[step, o], dst_ref=recv.at[step, source],
            send_sem=tile_send.at[step, o], recv_sem=tile_recv.at[step, source],
            device_id=place(o), device_id_type=MESH)

    def back_copy(step, o, source):
        return pltpu.make_async_remote_copy(
            src_ref=backsend.at[step, o], dst_ref=back.at[step, source],
            send_sem=back_send.at[step, o], recv_sem=back_recv.at[step, source],
            device_id=place(o), device_id_type=MESH)

    def run_step(step, carry):
        def fetch(o, put):
            for k in range(slots):
                at = k * n + o
                row = route_s[0, at]
                col = route_s[1, at]
                filled = (row >= 0).astype(f32)
                row = jnp.maximum(row, 0)
                col = jnp.maximum(col, 0)
                for c in range(3):
                    put(k * 3 + c, blocks[col, c, pl.ds(row, 1), :] * filled)

        top = pl.ds(8, 8)
        bottom = pl.ds(rows, 8)
        head = pl.ds(0, TILE)
        tail = pl.ds(cols - TILE, TILE)
        plans = (
            (colsend.at[step, 0], colrecv.at[step, 1], (gi, left)),
            (colsend.at[step, 1], colrecv.at[step, 0], (gi, right)),
            (xpad.at[:, top, pl.ds(0, cols)], rowrecv.at[step, 1], (up, gj)),
            (xpad.at[:, bottom, pl.ds(0, cols)], rowrecv.at[step, 0], (down, gj)),
            (xpad.at[:, bottom, tail], cornrecv.at[step, 0], (down, right)),
            (xpad.at[:, bottom, head], cornrecv.at[step, 1], (down, left)),
            (xpad.at[:, top, tail], cornrecv.at[step, 2], (up, right)),
            (xpad.at[:, top, head], cornrecv.at[step, 3], (up, left)),
        )
        halos = [
            pltpu.make_async_remote_copy(
                src_ref=src, dst_ref=dst, send_sem=halo_send.at[step, i], recv_sem=halo_recv.at[step, i],
                device_id=where, device_id_type=MESH)
            for i, (src, dst, where) in enumerate(plans)
        ]
        for copy in halos[2:]:
            copy.start()

        def send_tiles(d, carry):
            o = lax.rem(me + d, n)

            def put(j, value):
                sendbuf[step, o, pl.ds(j, 1), :] = value

            fetch(o, put)
            tile_copy(step, o, me).start()
            return carry

        lax.fori_loop(1, n, send_tiles, 0)

        def put_own(j, value):
            recv[step, me, pl.ds(j, 1), :] = value

        fetch(me, put_own)

        lane = lax.broadcasted_iota(jnp.int32, (rows, TILE), 1)
        packed = jnp.zeros((rows, TILE), f32)
        for c in range(3):
            first = pltpu.roll(xpad[c, 8:8 + rows, 0:TILE], 2 * c, 1) if c else xpad[c, 8:8 + rows, 0:TILE]
            last = pltpu.roll(xpad[c, 8:8 + rows, cols - TILE:cols], 10 + 2 * c, 1)
            packed = jnp.where((lane == 2 * c) | (lane == 2 * c + 1), first, packed)
            packed = jnp.where((lane == 8 + 2 * c) | (lane == 9 + 2 * c), last, packed)
        turned = jnp.transpose(packed)
        colsend[step, 0] = turned[0:8]
        colsend[step, 1] = turned[8:16]

        for copy in halos[:2]:
            copy.start()
        for copy in halos:
            copy.wait()

        joined = jnp.concatenate(
            [colrecv[step, 0], colrecv[step, 1], jnp.zeros((TILE - 16, rows), f32)], axis=0)
        sides = jnp.transpose(joined)
        lane8 = lax.broadcasted_iota(jnp.int32, (8, TILE), 1)
        for c in range(3):
            before = pltpu.roll(sides, 126 - 2 * c, 1) * has_left
            after = pltpu.roll(sides, 120 - 2 * c, 1) * has_right
            xpad[c, 8:8 + rows, cols:wide] = jnp.where(lane < 64, after, before)
            xpad[c, 0:8, 0:cols] = rowrecv[step, 0, c] * has_up
            xpad[c, 8 + rows:16 + rows, 0:cols] = rowrecv[step, 1, c] * has_down
            xpad[c, 0:8, cols:wide] = jnp.where(
                lane8 < 64, cornrecv[step, 1, c] * has_right, cornrecv[step, 0, c] * has_left) * has_up
            xpad[c, 8 + rows:16 + rows, cols:wide] = jnp.where(
                lane8 < 64, cornrecv[step, 3, c] * has_right, cornrecv[step, 2, c] * has_left) * has_down

        tall = CHUNK + 16

        def above(v):
            return pltpu.roll(v, 1, 0)

        def below(v):
            return pltpu.roll(v, tall - 1, 0)

        def before(v):
            return pltpu.roll(v, 1, 1)

        def after(v):
            return pltpu.roll(v, wide - 1, 1)

        def internal(chunk, carry):
            r0 = pl.multiple_of(chunk * CHUNK, CHUNK)
            x = [xpad[c, pl.ds(r0, tall), :] for c in range(3)]
            xa = [after(v) for v in x]
            xb = [below(v) for v in x]
            row = lax.broadcasted_iota(jnp.int32, (tall, wide), 0) + (r0 - 8)
            col = lax.broadcasted_iota(jnp.int32, (tall, wide), 1)
            mask = jnp.where(row < 0, has_up, jnp.where(row >= rows, has_down, 1.0))
            mask = mask * jnp.where(col == cols, has_right, jnp.where(col == wide - 1, has_left, 1.0))
            ea = [p - q for p, q in zip(xa, x)]
            eb = [p - q for p, q in zip(xb, x)]
            ga = 1.0 + hardening * (ea[0] * ea[0] + ea[1] * ea[1] + ea[2] * ea[2])
            gb = 1.0 + hardening * (eb[0] * eb[0] + eb[1] * eb[1] + eb[2] * eb[2])
            stiff = stiff_ref[pl.ds(r0, CHUNK), :]
            for c in range(3):
                fa = ea[c] * ga
                fb = eb[c] * gb
                pull = (fa - before(fa)) + (fb - above(fb))
                curve = ((ea[c] - before(ea[c])) + (eb[c] - above(eb[c]))) * mask
                bend = (above(curve) + below(curve)) + (before(curve) + after(curve)) - 4.0 * curve
                force[c, pl.ds(r0, CHUNK), :] = (
                    stiff * pull[8:8 + CHUNK, 0:cols] - bend_gain * bend[8:8 + CHUNK, 0:cols])
            return carry

        half = rows // CHUNK // 2
        lax.fori_loop(0, half, internal, 0)

        def tiles_in(d, carry):
            tile_copy(step, me, lax.rem(me + d, n)).wait_recv()
            return carry

        lax.fori_loop(1, n, tiles_in, 0)
        for k in range(slots):
            for c in range(3):
                rec8[k * n:(k + 1) * n, c, :] = recv[step, :, k * 3 + c, :] * SCALE

        def split_slots(g, carry):
            at = pl.ds(g * 8, 8)
            hi, mid, lo = split3(rec8[at])
            second = mid.astype(f32) + pltpu.roll(lo.astype(f32), 4, 1)
            aug[at] = jnp.concatenate([hi.astype(f32), second], axis=1).astype(bf16)
            return carry

        lax.fori_loop(0, total // 8, split_slots, 0)

        def sums(out):
            out = out[0:8] + out[8:16]
            return out + pltpu.roll(out, 4, 0)

        def slot_row(s):
            return lax.rem(s, slots) * n + lax.div(s, slots)

        def pairs(g, carry):
            for u in range(UNROLL):
                m = g * UNROLL + u
                a = slot_row(jnp.maximum(pair_s[0, m], 0))
                b = slot_row(jnp.maximum(pair_s[1, m], 0))
                p = jnp.transpose(rec8[a])
                q = rec8[b]
                his, los = [], []
                far = [jnp.zeros((8, TILE), f32) for c in range(3)]
                for r in range(0, TILE, BLOCK):
                    d = [p[r:r + BLOCK, c:c + 1] - q[c:c + 1, :] for c in range(3)]
                    w = jnp.exp2(-2.0 - (d[0] * d[0] + d[1] * d[1] + d[2] * d[2]))
                    hi = w.astype(bf16)
                    his.append(hi)
                    los.append((w - hi.astype(f32)).astype(bf16))
                    for c in range(3):
                        push = w * d[c]
                        for e in range(0, BLOCK, 8):
                            far[c] = far[c] + push[e:e + 8]
                qb = aug[b]
                qb = jnp.concatenate([qb, qb], axis=1)
                weights = jnp.concatenate(
                    [jnp.concatenate(his, axis=0), jnp.concatenate(los, axis=0)], axis=1)
                near = lax.dot_general(
                    qb, weights, (((1,), (1,)), ((), ())), preferred_element_type=f32)
                pairsum[m] = sums(near)
                for c in range(3):
                    pairsum[number + m, c:c + 1, :] = jnp.sum(far[c], axis=0, keepdims=True)
            return carry

        lax.fori_loop(0, number // UNROLL, pairs, 0)

        ids = lax.broadcasted_iota(jnp.int32, (total, number), 0)
        ids = lax.rem(ids, n) * slots + lax.div(ids, n)
        hot = jnp.concatenate(
            [(ids == pair_v[0:1, :]).astype(f32), (ids == pair_v[1:2, :]).astype(f32)], axis=1).astype(bf16)
        summed = []
        for c in range(4):
            parts = split3(pairsum[:, c, :])
            summed.append(sum(jnp.dot(hot, part, preferred_element_type=f32) for part in parts))
        for c in range(3):
            push = (rec8[:, c, :] * summed[3] - summed[c]) * (1.0 / SCALE)
            for k in range(slots):
                backsend[step, :, k * 3 + c, :] = push[k * n:(k + 1) * n]

        def send_back(d, carry):
            back_copy(step, lax.rem(me + d, n), me).start()
            return carry

        lax.fori_loop(1, n, send_back, 0)
        back[step, me] = backsend[step, me]
        lax.fori_loop(half, rows // CHUNK, internal, 0)

        def back_in(d, carry):
            back_copy(step, me, lax.rem(me + d, n)).wait_recv()
            return carry

        lax.fori_loop(1, n, back_in, 0)

        parts = [split3(jnp.concatenate([back[step, :, k * 3 + c, :] for k in range(slots)], axis=0))
                 for c in range(3)]
        parts = [jnp.concatenate([parts[c][i] for c in range(3)], axis=1) for i in range(3)]
        parts = jnp.concatenate(parts, axis=0)

        in_row = lax.broadcasted_iota(jnp.int32, (rows, total), 0) == route_v[0:1, :]
        for t in range(cols // TILE):
            at = slice(t * TILE, (t + 1) * TILE)
            hot = (in_row & (route_v[1:2, :] == t)).astype(f32).astype(bf16)
            hot = jnp.concatenate([hot, hot, hot], axis=1)
            contact = jnp.dot(hot, parts, preferred_element_type=f32)
            for c in range(3):
                v = vel_out[c, :, at]
                push = force[c, :, at] + contact[:, c * TILE:(c + 1) * TILE]
                v = v + time_step * (push - damping * v)
                x = xpad[c, 8:8 + rows, at] + time_step * v
                vel_out[c, :, at] = v
                xpad[c, 8:8 + rows, at] = x
                blocks[t, c] = x
                pos_out[c, :, at] = x

        def sent(d, carry):
            o = lax.rem(me + d, n)
            tile_copy(step, o, me).wait_send()
            back_copy(step, o, me).wait_send()
            return carry

        lax.fori_loop(1, n, sent, 0)
        return carry

    lax.fori_loop(0, STEPS, run_step, 0)


def local(ngx, ngy, positions, velocity, stiffness, send_tiles, pair_tiles):
    n = ngx * ngy
    rows, cols = stiffness.shape
    route = send_tiles.reshape(n, -1).T.reshape(-1)
    slots = route.shape[0] // n
    total = n * slots
    per_row = cols // TILE
    route = jnp.where(route >= 0, jnp.stack([route // per_row, route % per_row]), -1)
    paired = pair_tiles.reshape(2, -1)
    number = paired.shape[1]
    vmem = pl.BlockSpec(memory_space=pltpu.VMEM)
    smem = pl.BlockSpec(memory_space=pltpu.SMEM)
    dma = pltpu.SemaphoreType.DMA
    shape = jax.ShapeDtypeStruct(positions.shape, f32)
    return pl.pallas_call(
        functools.partial(kernel, ngx, ngy, slots),
        out_shape=(shape, shape),
        in_specs=[vmem, vmem, vmem, smem, vmem, smem, vmem],
        out_specs=(vmem, vmem),
        scratch_shapes=[
            pltpu.VMEM((3, rows + 16, cols + TILE), f32),
            pltpu.VMEM((cols // TILE, 3, rows, TILE), f32),
            pltpu.VMEM((3, rows, cols), f32),
            pltpu.VMEM((STEPS, n, slots * 3, TILE), f32),
            pltpu.VMEM((STEPS, n, slots * 3, TILE), f32),
            pltpu.VMEM((STEPS, n, slots * 3, TILE), f32),
            pltpu.VMEM((STEPS, n, slots * 3, TILE), f32),
            pltpu.VMEM((total, 8, TILE), f32),
            pltpu.VMEM((total, 16, TILE), bf16),
            pltpu.VMEM((2 * number, 8, TILE), f32),
            pltpu.VMEM((STEPS, 2, 8, rows), f32),
            pltpu.VMEM((STEPS, 2, 8, rows), f32),
            pltpu.VMEM((STEPS, 2, 3, 8, cols), f32),
            pltpu.VMEM((STEPS, 4, 3, 8, TILE), f32),
            dma((STEPS, n)), dma((STEPS, n)), dma((STEPS, n)), dma((STEPS, n)),
            dma((STEPS, 8)), dma((STEPS, 8)),
        ],
        compiler_params=pltpu.CompilerParams(
            collective_id=0, has_side_effects=True, vmem_limit_bytes=56 * 1024 * 1024),
        name="shell_steps",
    )(positions, velocity, stiffness, route, route, paired, paired)


def solution(mesh):
    ngx, ngy = mesh.shape["gx"], mesh.shape["gy"]
    return jax.shard_map(
        functools.partial(local, ngx, ngy),
        mesh=mesh,
        in_specs=(
            P(None, "gx", "gy"),
            P(None, "gx", "gy"),
            P("gx", "gy"),
            P("gx", "gy"),
            P("gx", "gy", None, None),
        ),
        out_specs=(P(None, "gx", "gy"), P(None, "gx", "gy")),
        check_vma=False,
    )
```
